32 devices in a mesh: site: 8 (over z, x), sector: 4 (over y, core).
Axes of the slice: x: 2, y: 2, z: 4, core: 2. Of those that a mesh axis runs over, the one named last changes fastest.
Arguments:
- site_tensors: bfloat16 [8, 2, 1536, 384], P('site', None, 'sector'), may hold values from -0.21875 to 0.21875
- environments: bfloat16 [8, 5, 1536, 384], P('site', None, 'sector'), may hold values from -6 to 6
- mpo: float32 [8, 5, 5, 2, 2], P('site'), may hold values from -4 to 4
- boundary: bfloat16 [5, 1536, 384], P(None, 'sector'), may hold values from -6 to 6
Outputs:
- environments_out: bfloat16 [8, 5, 1536, 384], P('site', None, 'sector')
The draws below stay inside these ranges and needn't reach their ends.
All inputs are finite; a program needn't handle non-finite values.
Results may differ from the reference program's by a relative error of at most 0.0054.
Values may be sent and summed in bfloat16 or wider, within the bound.
A program may use at most 64 MiB of HBM per device.

```python
import jax
import jax.numpy as jnp
import numpy as np
from jax import lax

SEC = 384
W = 5
TICKS = 1
NSEC = 4
CHI = 1536
SITES = 8


def block_levels(key, shape, shards, low, largest):
    factor_of, own = 1.0, jax.random.fold_in(key, 6)
    for dim, shards_of in shards:
        draws = jnp.exp(jax.random.uniform(jax.random.fold_in(own, dim), (shards_of,), jnp.float32, low / len(shards), largest / len(shards)))
        factor_of = factor_of * jnp.repeat(draws, shape[dim] // shards_of).reshape([-1 if axis == dim else 1 for axis in range(len(shape))])
    return factor_of


def normal_values(rng, shape, spread, bound, pieces=(), kind=jnp.bfloat16):
    values = spread * jax.random.normal(rng, shape, jnp.float32)
    if pieces:
        values = values * block_levels(rng, shape, pieces, -0.22, 0.18)
    return jnp.clip(values, -bound, bound).astype(kind)


def setup_inputs(seed: int = 0) -> dict:
    key_list = jax.random.split(jax.random.key(seed), 5)
    return {
        "site_tensors": normal_values(key_list[0], (SITES, 2, CHI, SEC), (2 * SEC) ** -0.5, 0.21875, ((0, 8), (2, 4))),
        "environments": normal_values(key_list[1], (SITES, W, CHI, SEC), 1.0, 6.0, ((0, 8), (2, 4))),
        "mpo": normal_values(key_list[2], (SITES, W, W, 2, 2), 0.6, 4.0, ((0, 8),), jnp.float32),
        "boundary": normal_values(key_list[3], (W, CHI, SEC), 1.0, 6.0, ((1, 4),)),
    }


charge_steps = (0, 1, -1, 0, 0)


def allowed():
    charges = np.array(charge_steps)
    spins = np.arange(2)
    differ = charges[None, :] - charges[:, None]
    return (spins[None, None, None, :] - spins[None, None, :, None] == differ[:, :, None, None]).astype(np.float32)


def transfer(incoming, blocks, weights):
    env_blocks = incoming.reshape(W, NSEC, SEC, SEC).astype(jnp.float32)
    site_blocks = blocks.reshape(2, NSEC, SEC, SEC).astype(jnp.float32)
    rolled = jnp.stack([jnp.roll(site_blocks, -charge_steps[term], axis=1) for term in range(W)])
    products = jnp.einsum('wqab,wtqbc->wtqac', env_blocks, rolled)
    couplings = weights * jnp.asarray(allowed(), weights.dtype)
    combined = jnp.einsum('wvst,wtqac->vsqac', couplings, products, precision=lax.Precision.HIGHEST).astype(jnp.bfloat16)
    halves = jnp.einsum('sqba,vsqbc->vsqac', site_blocks, combined.astype(jnp.float32))
    carried = lax.optimization_barrier(halves[:, 1].astype(jnp.bfloat16))
    carried = jnp.roll(carried.astype(jnp.float32), 1, axis=1)
    updated = (halves[:, 0] + carried).astype(jnp.bfloat16)
    return updated.reshape(W, CHI, SEC)


def reference(site_tensors, environments, mpo, boundary):
    state = environments
    for tick_index in range(TICKS):
        incoming = jnp.concatenate([boundary[None], state[:-1]], axis=0)
        state = lax.map(lambda item: transfer(item[0], item[1], item[2]), (incoming, site_tensors, mpo))
    return state
```

```python
import functools

import jax
import jax.numpy as jnp
from jax import lax
from jax.experimental import pallas as pl
from jax.experimental.pallas import tpu as pltpu
from jax.sharding import PartitionSpec as P

MESH = pl.DeviceIdType.MESH
charge_steps = (0, 1, -1, 0, 0)
W = len(charge_steps)
ORDER = (1, 0, 3, 4, 2)
DEPTH = 2


def targets(w, t):
    return [
        (v, s)
        for v in range(W)
        for s in range(2)
        if t - s == charge_steps[v] - charge_steps[w]
    ]


def dot(a, b):
    return jnp.dot(a, b, preferred_element_type=jnp.float32)


def kernel(
    ns, nq, site, env, mpo, bnd, out,
    inc, near, flip, total, carry_out, carry_in,
    env_send, env_recv, near_send, near_recv, carry_send, carry_recv, local_sem,
):
    s = lax.axis_index("site")
    q = lax.axis_index("sector")
    nxt, prv = lax.rem(s + 1, ns), lax.rem(s + ns - 1, ns)
    above, below = lax.rem(q + 1, nq), lax.rem(q + nq - 1, nq)
    has_next, has_prev = s < ns - 1, s > 0

    barrier = pltpu.get_barrier_semaphore()
    for other in (above, below):
        pl.semaphore_signal(barrier, inc=1, device_id={"site": s, "sector": other}, device_id_type=MESH)

    @pl.when(has_next)
    def _():
        pl.semaphore_signal(barrier, inc=1, device_id={"site": nxt, "sector": q}, device_id_type=MESH)

    @pl.when(has_prev)
    def _():
        pl.semaphore_signal(barrier, inc=1, device_id={"site": prv, "sector": q}, device_id_type=MESH)

    pl.semaphore_wait(barrier, 2 + has_next.astype(jnp.int32) + has_prev.astype(jnp.int32))

    def env_copy(k):
        w = ORDER[k]
        return pltpu.make_async_remote_copy(
            src_ref=env.at[0, w], dst_ref=inc.at[w],
            send_sem=env_send.at[k], recv_sem=env_recv.at[k],
            device_id={"site": nxt, "sector": q}, device_id_type=MESH,
        )

    def start_env(k):
        @pl.when(has_next)
        def _():
            env_copy(k).start()

    near_copies = [
        pltpu.make_async_remote_copy(
            src_ref=site.at[0], dst_ref=near.at[i],
            send_sem=near_send.at[i], recv_sem=near_recv.at[i],
            device_id={"site": s, "sector": other}, device_id_type=MESH,
        )
        for i, other in ((0, above), (1, below))
    ]
    carry_copies = [
        pltpu.make_async_remote_copy(
            src_ref=carry_out.at[v], dst_ref=carry_in.at[v],
            send_sem=carry_send.at[v], recv_sem=carry_recv.at[v],
            device_id={"site": s, "sector": above}, device_id_type=MESH,
        )
        for v in range(W)
    ]

    for k in range(DEPTH):
        start_env(k)
    near_copies[1].start()
    near_copies[0].start()

    @pl.when(jnp.logical_not(has_prev))
    def _():
        copy = pltpu.make_async_copy(bnd, inc, local_sem)
        copy.start()
        copy.wait()

    for t in range(2):
        flip[t] = site[0, t].T

    left = {(v, x): sum((v, x) in targets(w, t) for w in range(W) for t in range(2)) for v in range(W) for x in range(2)}
    begun, seen = set(), set()
    for k, w in enumerate(ORDER):
        if k + DEPTH <= W - 1:
            @pl.when(has_next)
            def _():
                env_copy(k).wait_send()
                env_copy(k + DEPTH).start()

        @pl.when(has_prev)
        def _():
            env_copy(k).wait_recv()

        step = charge_steps[w]
        if step and step not in seen:
            near_copies[(step + 1) // 2].wait_recv()
            seen.add(step)
        done = []
        for t in (1, 0):
            block = site[0, t] if step == 0 else near[(step + 1) // 2, t]
            product = dot(inc[w], block)
            for v, x in targets(w, t):
                term = mpo[0, w, v, x, t] * product
                if (v, x) in begun:
                    total[v, x] += term
                else:
                    total[v, x] = term
                    begun.add((v, x))
                left[v, x] -= 1
                if not left[v, x]:
                    done.append((v, x))
        for v, x in sorted(done, key=lambda item: -item[1]):
            part = dot(flip[x], total[v, x].astype(jnp.bfloat16))
            if x:
                carry_out[v] = part.astype(jnp.bfloat16)
                carry_copies[v].start()
            else:
                total[v, 0] = part

    for v in (1, 0, 3, 4, 2):
        carry_copies[v].wait_recv()
        out[0, v] = (total[v, 0] + carry_in[v].astype(jnp.float32)).astype(jnp.bfloat16)

    for copy in near_copies + carry_copies:
        copy.wait_send()

    @pl.when(has_next)
    def _():
        for k in range(W - DEPTH, W):
            env_copy(k).wait_send()


def solution(mesh):
    ns, nq = mesh.shape["site"], mesh.shape["sector"]

    def local(site_tensors, environments, mpo, boundary):
        width = site_tensors.shape[3]
        vmem = functools.partial(pltpu.VMEM)
        dma = pltpu.SemaphoreType.DMA
        bf16, f32 = jnp.bfloat16, jnp.float32
        return pl.pallas_call(
            functools.partial(kernel, ns, nq),
            out_shape=jax.ShapeDtypeStruct(environments.shape, bf16),
            in_specs=[
                pl.BlockSpec(memory_space=pltpu.VMEM),
                pl.BlockSpec(memory_space=pl.ANY),
                pl.BlockSpec(memory_space=pltpu.SMEM),
                pl.BlockSpec(memory_space=pl.ANY),
            ],
            out_specs=pl.BlockSpec(memory_space=pltpu.VMEM),
            scratch_shapes=[
                vmem((W, width, width), bf16),
                vmem((2, 2, width, width), bf16),
                vmem((2, width, width), bf16),
                vmem((W, 2, width, width), f32),
                vmem((W, width, width), bf16),
                vmem((W, width, width), bf16),
                dma((W,)), dma((W,)), dma((2,)), dma((2,)), dma((W,)), dma((W,)), dma,
            ],
            compiler_params=pltpu.CompilerParams(
                collective_id=0, has_side_effects=True, vmem_limit_bytes=48 * 2**20
            ),
            cost_estimate=pl.CostEstimate(
                flops=40 * width**3, bytes_accessed=24 * W * width * width, transcendentals=0
            ),
        )(site_tensors, environments, mpo, boundary)

    return jax.shard_map(
        local,
        mesh=mesh,
        in_specs=(
            P("site", None, "sector", None),
            P("site", None, "sector", None),
            P("site", None, None, None, None),
            P(None, "sector", None),
        ),
        out_specs=P("site", None, "sector", None),
        check_vma=False,
    )
```

```python
import functools

import jax
import jax.numpy as jnp
from jax import lax
from jax.experimental import pallas as pl
from jax.experimental.pallas import tpu as pltpu
from jax.sharding import PartitionSpec as P

MESH = pl.DeviceIdType.MESH
charge_steps = (0, 1, -1, 0, 0)
W = len(charge_steps)
ORDER = (1, 2, 0, 3, 4)
DEPTH = 2


def uses(w, t, x):
    return [v for v in range(W) if t - x == charge_steps[v] - charge_steps[w]]


def dot(a, b):
    return jnp.dot(a, b, preferred_element_type=jnp.float32)


def chunks_of(width):
    whole = [(w, 0, width) for w in ORDER[:-1]]
    cut = width - max(width // 3, 16)
    return whole + [(ORDER[-1], 0, cut), (ORDER[-1], cut, width - cut)]


def kernel(
    ns, nq, site_hbm, env, mpo, bnd, out,
    site, inc, low, below_site, above_site, flip, total, part, pair_out,
    env_send, env_recv, relay_send, relay_recv, near_send, near_recv, local_sem,
):
    s = lax.axis_index("site")
    q = lax.axis_index("sector")
    nxt, prv = lax.rem(s + 1, ns), lax.rem(s + ns - 1, ns)
    above, below = lax.rem(q + 1, nq), lax.rem(q + nq - 1, nq)
    has_next, has_prev = s < ns - 1, s > 0
    width = site.shape[-1]
    chunks = chunks_of(width)
    count = len(chunks)

    def at(place, sector):
        return {"site": place, "sector": sector}

    own_copy = pltpu.make_async_copy(site_hbm.at[0], site, local_sem.at[0])
    own_copy.start()
    bnd_copy = pltpu.make_async_copy(bnd, inc, local_sem.at[1])

    @pl.when(jnp.logical_not(has_prev))
    def _():
        bnd_copy.start()

    barrier = pltpu.get_barrier_semaphore()
    for other in (above, below):
        pl.semaphore_signal(barrier, inc=1, device_id=at(s, other), device_id_type=MESH)

    @pl.when(has_next)
    def _():
        pl.semaphore_signal(barrier, inc=1, device_id=at(nxt, q), device_id_type=MESH)

    @pl.when(has_prev)
    def _():
        pl.semaphore_signal(barrier, inc=1, device_id=at(prv, q), device_id_type=MESH)

    pl.semaphore_wait(barrier, 2 + has_next.astype(jnp.int32) + has_prev.astype(jnp.int32))

    def env_copy(k):
        w, row, rows = chunks[k]
        return pltpu.make_async_remote_copy(
            src_ref=env.at[0, w, pl.ds(row, rows)], dst_ref=inc.at[w, pl.ds(row, rows)],
            send_sem=env_send.at[k], recv_sem=env_recv.at[k],
            device_id=at(nxt, q), device_id_type=MESH,
        )

    def relay_copy(k):
        w, row, rows = chunks[k]
        source = pair_out if charge_steps[w] < 0 else inc.at[w, pl.ds(row, rows)]
        return pltpu.make_async_remote_copy(
            src_ref=source, dst_ref=low.at[w, pl.ds(row, rows)],
            send_sem=relay_send.at[k], recv_sem=relay_recv.at[k],
            device_id=at(s, above), device_id_type=MESH,
        )

    to_below = pltpu.make_async_remote_copy(
        src_ref=site_hbm.at[0, 0], dst_ref=above_site,
        send_sem=near_send.at[0], recv_sem=near_recv.at[0],
        device_id=at(s, below), device_id_type=MESH,
    )
    to_above = pltpu.make_async_remote_copy(
        src_ref=site_hbm.at[0], dst_ref=below_site,
        send_sem=near_send.at[1], recv_sem=near_recv.at[1],
        device_id=at(s, above), device_id_type=MESH,
    )

    @pl.when(has_next)
    def _():
        for k in range(DEPTH):
            env_copy(k).start()

    to_below.start()
    to_above.start()

    own_copy.wait()
    flip[0] = site[0].T

    @pl.when(jnp.logical_not(has_prev))
    def _():
        bnd_copy.wait()

    begun = set()
    left = {
        (v, x): sum(v in uses(w, t, x) for w in range(W) for t in range(2))
        for v in range(W) for x in range(2)
    }

    def add(product, k, t, x):
        w, row, rows = chunks[k]
        final = row + rows == width
        for v in uses(w, t, x):
            term = mpo[0, w, x, t, v] * product
            last = left[v, x] == 1
            if final:
                left[v, x] -= 1
            if (v, x) in begun:
                term = total[v, x, row:row + rows] + term
            if last:
                piece = dot(flip[x, :, row:row + rows], term.astype(jnp.bfloat16))
                if row:
                    piece = part[v, x] + piece
                if x and w == ORDER[-1] and final:
                    carried = piece.astype(jnp.bfloat16).astype(jnp.float32)
                    out[0, v] = (part[v, 0] + carried).astype(jnp.bfloat16)
                else:
                    part[v, x] = piece
            else:
                total[v, x, row:row + rows] = term
                if final:
                    begun.add((v, x))

    def own(k):
        w, row, rows = chunks[k]
        step = charge_steps[w]
        rows_in = inc[w, row:row + rows]
        for t in (1, 0):
            if not uses(w, t, 0) and not (step < 0 and t == 1):
                continue
            block = site[t] if step == 0 else above_site[...] if step > 0 else below_site[t]
            product = dot(rows_in, block)
            if step < 0 and t == 1:
                pair_out[...] = product.astype(jnp.bfloat16)
                relay_copy(k).start()
            add(product, k, t, 0)

    def lower(k):
        w, row, rows = chunks[k]
        step = charge_steps[w]
        relay_copy(k).wait_recv()
        rows_in = low[w, row:row + rows]
        if step < 0:
            add(rows_in.astype(jnp.float32), k, 1, 1)
            return
        for t in (1, 0):
            if uses(w, t, 1):
                add(dot(rows_in, below_site[t] if step == 0 else site[t]), k, t, 1)

    for k, (w, row, rows) in enumerate(chunks):
        @pl.when(has_prev)
        def _():
            env_copy(k).wait_recv()

        if charge_steps[w] >= 0:
            relay_copy(k).start()

        if k + DEPTH < count:
            @pl.when(has_next)
            def _():
                env_copy(k).wait_send()
                env_copy(k + DEPTH).start()

        if k == 0:
            to_below.wait_recv()
            to_above.wait_recv()
            flip[1] = below_site[1].T
        own(k)
        if k:
            lower(k - 1)
    carried = part[1, 1].astype(jnp.bfloat16).astype(jnp.float32)
    out[0, 1] = (part[1, 0] + carried).astype(jnp.bfloat16)
    lower(count - 1)

    to_below.wait_send()
    to_above.wait_send()
    for k in range(count):
        relay_copy(k).wait_send()

    @pl.when(has_next)
    def _():
        for k in range(count - DEPTH, count):
            env_copy(k).wait_send()


def solution(mesh):
    ns, nq = mesh.shape["site"], mesh.shape["sector"]

    def local(site_tensors, environments, mpo, boundary):
        width = site_tensors.shape[3]
        count = len(chunks_of(width))
        vmem, dma = pltpu.VMEM, pltpu.SemaphoreType.DMA
        bf16, f32 = jnp.bfloat16, jnp.float32
        return pl.pallas_call(
            functools.partial(kernel, ns, nq),
            out_shape=jax.ShapeDtypeStruct(environments.shape, bf16),
            in_specs=[
                pl.BlockSpec(memory_space=pltpu.HBM),
                pl.BlockSpec(memory_space=pltpu.HBM),
                pl.BlockSpec(memory_space=pltpu.SMEM),
                pl.BlockSpec(memory_space=pltpu.HBM),
            ],
            out_specs=pl.BlockSpec(memory_space=pltpu.VMEM),
            scratch_shapes=[
                vmem((2, width, width), bf16),
                vmem((W, width, width), bf16),
                vmem((W, width, width), bf16),
                vmem((2, width, width), bf16),
                vmem((width, width), bf16),
                vmem((2, width, width), bf16),
                vmem((W, 2, width, width), f32),
                vmem((W, 2, width, width), f32),
                vmem((width, width), bf16),
                dma((count,)), dma((count,)), dma((count,)), dma((count,)),
                dma((2,)), dma((2,)), dma((2,)),
            ],
            compiler_params=pltpu.CompilerParams(
                collective_id=0, has_side_effects=True, vmem_limit_bytes=60 * 2**20
            ),
            cost_estimate=pl.CostEstimate(
                flops=54 * width**3, bytes_accessed=24 * W * width * width, transcendentals=0
            ),
        )(site_tensors, environments, mpo.transpose(0, 1, 3, 4, 2), boundary)

    return jax.shard_map(
        local,
        mesh=mesh,
        in_specs=(
            P("site", None, "sector", None),
            P("site", None, "sector", None),
            P("site", None, None, None, None),
            P(None, "sector", None),
        ),
        out_specs=P("site", None, "sector", None),
        check_vma=False,
    )
```

```python
import functools

import jax
import jax.numpy as jnp
from jax import lax
from jax.experimental import pallas as pl
from jax.experimental.pallas import tpu as pltpu
from jax.sharding import PartitionSpec as P

MESH = pl.DeviceIdType.MESH
charge_steps = (0, 1, -1, 0, 0)
W = len(charge_steps)
ORDER = (1, 2, 0, 3, 4)
DEPTH = 3


def uses(w, t, x):
    return [v for v in range(W) if t - x == charge_steps[v] - charge_steps[w]]


def dot(a, b):
    return jnp.dot(a, b, preferred_element_type=jnp.float32)


def chunks_of(width):
    cut = width - width // 3
    return [(w, 0, cut) for w in ORDER] + [(w, cut, width - cut) for w in ORDER]


def kernel(
    ns, nq, site_hbm, env, mpo, bnd, out,
    site, inc, low, below_site, above_site, flip, total, part, pair_out,
    env_send, env_recv, relay_send, relay_recv, near_send, near_recv, local_sem,
):
    s = lax.axis_index("site")
    q = lax.axis_index("sector")
    nxt, prv = lax.rem(s + 1, ns), lax.rem(s + ns - 1, ns)
    above, below = lax.rem(q + 1, nq), lax.rem(q + nq - 1, nq)
    has_next, has_prev = s < ns - 1, s > 0
    width = site.shape[-1]
    chunks = chunks_of(width)
    count = len(chunks)

    def at(place, sector):
        return {"site": place, "sector": sector}

    own_copy = pltpu.make_async_copy(site_hbm.at[0], site, local_sem.at[0])
    own_copy.start()
    bnd_copy = pltpu.make_async_copy(bnd, inc, local_sem.at[1])

    @pl.when(jnp.logical_not(has_prev))
    def _():
        bnd_copy.start()

    barrier = pltpu.get_barrier_semaphore()
    for other in (above, below):
        pl.semaphore_signal(barrier, inc=1, device_id=at(s, other), device_id_type=MESH)

    @pl.when(has_next)
    def _():
        pl.semaphore_signal(barrier, inc=1, device_id=at(nxt, q), device_id_type=MESH)

    @pl.when(has_prev)
    def _():
        pl.semaphore_signal(barrier, inc=1, device_id=at(prv, q), device_id_type=MESH)

    pl.semaphore_wait(barrier, 2 + has_next.astype(jnp.int32) + has_prev.astype(jnp.int32))

    def env_copy(k):
        w, row, rows = chunks[k]
        return pltpu.make_async_remote_copy(
            src_ref=env.at[0, w, pl.ds(row, rows)], dst_ref=inc.at[w, pl.ds(row, rows)],
            send_sem=env_send.at[k], recv_sem=env_recv.at[k],
            device_id=at(nxt, q), device_id_type=MESH,
        )

    def relay_copy(k):
        w, row, rows = chunks[k]
        source = (pair_out if charge_steps[w] < 0 else inc.at[w]).at[pl.ds(row, rows)]
        return pltpu.make_async_remote_copy(
            src_ref=source, dst_ref=low.at[w, pl.ds(row, rows)],
            send_sem=relay_send.at[k], recv_sem=relay_recv.at[k],
            device_id=at(s, above), device_id_type=MESH,
        )

    to_below = pltpu.make_async_remote_copy(
        src_ref=site_hbm.at[0, 0], dst_ref=above_site,
        send_sem=near_send.at[0], recv_sem=near_recv.at[0],
        device_id=at(s, below), device_id_type=MESH,
    )
    to_above = pltpu.make_async_remote_copy(
        src_ref=site_hbm.at[0], dst_ref=below_site,
        send_sem=near_send.at[1], recv_sem=near_recv.at[1],
        device_id=at(s, above), device_id_type=MESH,
    )

    @pl.when(has_next)
    def _():
        for k in range(DEPTH):
            env_copy(k).start()

    to_below.start()
    to_above.start()

    own_copy.wait()
    flip[0] = site[0].T

    @pl.when(jnp.logical_not(has_prev))
    def _():
        bnd_copy.wait()

    seen, complete = {}, set()
    needed = {
        (v, x): sum(v in uses(w, t, x) for w in range(W) for t in range(2))
        for v in range(W) for x in range(2)
    }

    def add(product, k, t, x):
        w, row, rows = chunks[k]
        for v in uses(w, t, x):
            term = mpo[0, w, x, t, v] * product
            so_far = seen.get((v, x, row), 0)
            seen[v, x, row] = so_far + 1
            if so_far:
                term = total[v, x, row:row + rows] + term
            if so_far + 1 < needed[v, x]:
                total[v, x, row:row + rows] = term
                continue
            piece = dot(flip[x, :, row:row + rows], term.astype(jnp.bfloat16))
            if row:
                piece = part[v, x] + piece
            if row and v in complete:
                own_piece, carried = (part[v, 0], piece) if x else (piece, part[v, 1])
                carried = carried.astype(jnp.bfloat16).astype(jnp.float32)
                out[0, v] = (own_piece + carried).astype(jnp.bfloat16)
                continue
            part[v, x] = piece
            if row:
                complete.add(v)

    def own(k):
        w, row, rows = chunks[k]
        step = charge_steps[w]
        rows_in = inc[w, row:row + rows]
        for t in (1, 0):
            if not uses(w, t, 0) and not (step < 0 and t == 1):
                continue
            block = site[t] if step == 0 else above_site[...] if step > 0 else below_site[t]
            product = dot(rows_in, block)
            if step < 0 and t == 1:
                pair_out[row:row + rows] = product.astype(jnp.bfloat16)
                relay_copy(k).start()
            add(product, k, t, 0)

    def lower(k):
        w, row, rows = chunks[k]
        step = charge_steps[w]
        relay_copy(k).wait_recv()
        rows_in = low[w, row:row + rows]
        if step < 0:
            add(rows_in.astype(jnp.float32), k, 1, 1)
            return
        for t in (1, 0):
            if uses(w, t, 1):
                add(dot(rows_in, below_site[t] if step == 0 else site[t]), k, t, 1)

    for k, (w, row, rows) in enumerate(chunks):
        @pl.when(has_prev)
        def _():
            env_copy(k).wait_recv()

        if charge_steps[w] >= 0:
            relay_copy(k).start()

        if k + DEPTH < count:
            @pl.when(has_next)
            def _():
                env_copy(k).wait_send()
                env_copy(k + DEPTH).start()

        if k == 0:
            to_below.wait_recv()
            to_above.wait_recv()
            flip[1] = below_site[1].T
        own(k)
        if k:
            lower(k - 1)
    lower(count - 1)

    to_below.wait_send()
    to_above.wait_send()
    for k in range(count):
        relay_copy(k).wait_send()

    @pl.when(has_next)
    def _():
        for k in range(count - DEPTH, count):
            env_copy(k).wait_send()


def solution(mesh):
    ns, nq = mesh.shape["site"], mesh.shape["sector"]

    def local(site_tensors, environments, mpo, boundary):
        width = site_tensors.shape[3]
        count = len(chunks_of(width))
        vmem, dma = pltpu.VMEM, pltpu.SemaphoreType.DMA
        bf16, f32 = jnp.bfloat16, jnp.float32
        return pl.pallas_call(
            functools.partial(kernel, ns, nq),
            out_shape=pltpu.VMEM(environments.shape, bf16),
            in_specs=[
                pl.BlockSpec(memory_space=pltpu.HBM),
                pl.BlockSpec(memory_space=pltpu.HBM),
                pl.BlockSpec(memory_space=pltpu.SMEM),
                pl.BlockSpec(memory_space=pltpu.HBM),
            ],
            out_specs=pl.BlockSpec(memory_space=pltpu.VMEM),
            scratch_shapes=[
                vmem((2, width, width), bf16),
                vmem((W, width, width), bf16),
                vmem((W, width, width), bf16),
                vmem((2, width, width), bf16),
                vmem((width, width), bf16),
                vmem((2, width, width), bf16),
                vmem((W, 2, width, width), f32),
                vmem((W, 2, width, width), f32),
                vmem((width, width), bf16),
                dma((count,)), dma((count,)), dma((count,)), dma((count,)),
                dma((2,)), dma((2,)), dma((2,)),
            ],
            compiler_params=pltpu.CompilerParams(
                collective_id=0, has_side_effects=True, vmem_limit_bytes=60 * 2**20
            ),
            cost_estimate=pl.CostEstimate(
                flops=54 * width**3, bytes_accessed=24 * W * width * width, transcendentals=0
            ),
        )(site_tensors, environments, mpo.transpose(0, 1, 3, 4, 2), boundary)

    return jax.shard_map(
        local,
        mesh=mesh,
        in_specs=(
            P("site", None, "sector", None),
            P("site", None, "sector", None),
            P("site", None, None, None, None),
            P(None, "sector", None),
        ),
        out_specs=P("site", None, "sector", None),
        check_vma=False,
    )
```

```python
import functools

import jax
import jax.numpy as jnp
from jax import lax
from jax.experimental import pallas as pl
from jax.experimental.pallas import tpu as pltpu
from jax.sharding import PartitionSpec as P

MESH = pl.DeviceIdType.MESH
charge_steps = (0, 1, -1, 0, 0)
W = len(charge_steps)
ORDER = (1, 0, 3, 4, 2)
DEPTH = 3


def uses(w, t, x):
    return [v for v in range(W) if t - x == charge_steps[v] - charge_steps[w]]


def dot(a, b):
    return jnp.dot(a, b, preferred_element_type=jnp.float32)


def chunks_of(width):
    cut = width - width // 3
    return [(w, 0, cut) for w in ORDER] + [(w, cut, width - cut) for w in ORDER]


def kernel(
    ns, nq, site_hbm, env, mpo, bnd, out,
    site, inc, low, below_site, above_site, flip, total, part, pair_out,
    env_send, env_recv, relay_send, relay_recv, near_send, near_recv, local_sem,
):
    s = lax.axis_index("site")
    q = lax.axis_index("sector")
    nxt, prv = lax.rem(s + 1, ns), lax.rem(s + ns - 1, ns)
    above, below = lax.rem(q + 1, nq), lax.rem(q + nq - 1, nq)
    has_next, has_prev = s < ns - 1, s > 0
    width = site.shape[-1]
    chunks = chunks_of(width)
    count = len(chunks)

    def at(place, sector):
        return {"site": place, "sector": sector}

    own_copy = pltpu.make_async_copy(site_hbm.at[0], site, local_sem.at[0])
    own_copy.start()
    bnd_copy = pltpu.make_async_copy(bnd, inc, local_sem.at[1])

    @pl.when(jnp.logical_not(has_prev))
    def _():
        bnd_copy.start()

    barrier = pltpu.get_barrier_semaphore()
    for other in (above, below):
        pl.semaphore_signal(barrier, inc=1, device_id=at(s, other), device_id_type=MESH)

    @pl.when(has_next)
    def _():
        pl.semaphore_signal(barrier, inc=1, device_id=at(nxt, q), device_id_type=MESH)

    @pl.when(has_prev)
    def _():
        pl.semaphore_signal(barrier, inc=1, device_id=at(prv, q), device_id_type=MESH)

    pl.semaphore_wait(barrier, 2 + has_next.astype(jnp.int32) + has_prev.astype(jnp.int32))

    def env_copy(k):
        w, row, rows = chunks[k]
        return pltpu.make_async_remote_copy(
            src_ref=env.at[0, w, pl.ds(row, rows)], dst_ref=inc.at[w, pl.ds(row, rows)],
            send_sem=env_send.at[k], recv_sem=env_recv.at[k],
            device_id=at(nxt, q), device_id_type=MESH,
        )

    def relay_copy(k):
        w, row, rows = chunks[k]
        source = (pair_out if charge_steps[w] < 0 else inc.at[w]).at[pl.ds(row, rows)]
        return pltpu.make_async_remote_copy(
            src_ref=source, dst_ref=low.at[w, pl.ds(row, rows)],
            send_sem=relay_send.at[k], recv_sem=relay_recv.at[k],
            device_id=at(s, above), device_id_type=MESH,
        )

    to_below = pltpu.make_async_remote_copy(
        src_ref=site_hbm.at[0, 0], dst_ref=above_site,
        send_sem=near_send.at[0], recv_sem=near_recv.at[0],
        device_id=at(s, below), device_id_type=MESH,
    )
    to_above = pltpu.make_async_remote_copy(
        src_ref=site_hbm.at[0], dst_ref=below_site,
        send_sem=near_send.at[1], recv_sem=near_recv.at[1],
        device_id=at(s, above), device_id_type=MESH,
    )

    @pl.when(has_next)
    def _():
        for k in range(DEPTH):
            env_copy(k).start()

    to_below.start()
    to_above.start()

    own_copy.wait()
    flip[0] = site[0].T

    @pl.when(jnp.logical_not(has_prev))
    def _():
        bnd_copy.wait()

    seen, complete = {}, set()
    needed = {
        (v, x): sum(v in uses(w, t, x) for w in range(W) for t in range(2))
        for v in range(W) for x in range(2)
    }

    def add(product, k, t, x):
        w, row, rows = chunks[k]
        for v in uses(w, t, x):
            term = mpo[0, w, x, t, v] * product
            so_far = seen.get((v, x, row), 0)
            seen[v, x, row] = so_far + 1
            if so_far:
                term = total[v, x, row:row + rows] + term
            if so_far + 1 < needed[v, x]:
                total[v, x, row:row + rows] = term
                continue
            piece = dot(flip[x, :, row:row + rows], term.astype(jnp.bfloat16))
            if row:
                piece = part[v, x] + piece
            if row and v in complete:
                own_piece, carried = (part[v, 0], piece) if x else (piece, part[v, 1])
                carried = carried.astype(jnp.bfloat16).astype(jnp.float32)
                out[0, v] = (own_piece + carried).astype(jnp.bfloat16)
                continue
            part[v, x] = piece
            if row:
                complete.add(v)

    def own(k):
        w, row, rows = chunks[k]
        step = charge_steps[w]
        rows_in = inc[w, row:row + rows]
        for t in (1, 0):
            if not uses(w, t, 0) and not (step < 0 and t == 1):
                continue
            block = site[t] if step == 0 else above_site[...] if step > 0 else below_site[t]
            product = dot(rows_in, block)
            if step < 0 and t == 1:
                pair_out[row:row + rows] = product.astype(jnp.bfloat16)
                relay_copy(k).start()
            add(product, k, t, 0)

    def lower(k):
        w, row, rows = chunks[k]
        step = charge_steps[w]
        relay_copy(k).wait_recv()
        rows_in = low[w, row:row + rows]
        if step < 0:
            add(rows_in.astype(jnp.float32), k, 1, 1)
            return
        for t in (1, 0):
            if uses(w, t, 1):
                add(dot(rows_in, below_site[t] if step == 0 else site[t]), k, t, 1)

    for k, (w, row, rows) in enumerate(chunks):
        @pl.when(has_prev)
        def _():
            env_copy(k).wait_recv()

        if charge_steps[w] >= 0:
            relay_copy(k).start()

        if k + DEPTH < count:
            @pl.when(has_next)
            def _():
                env_copy(k).wait_send()
                env_copy(k + DEPTH).start()

        if k == 0:
            to_below.wait_recv()
            to_above.wait_recv()
            flip[1] = below_site[1].T
        own(k)
        if k:
            lower(k - 1)
    lower(count - 1)

    to_below.wait_send()
    to_above.wait_send()
    for k in range(count):
        relay_copy(k).wait_send()

    @pl.when(has_next)
    def _():
        for k in range(count - DEPTH, count):
            env_copy(k).wait_send()


def solution(mesh):
    ns, nq = mesh.shape["site"], mesh.shape["sector"]

    def local(site_tensors, environments, mpo, boundary):
        width = site_tensors.shape[3]
        count = len(chunks_of(width))
        vmem, dma = pltpu.VMEM, pltpu.SemaphoreType.DMA
        bf16, f32 = jnp.bfloat16, jnp.float32
        return pl.pallas_call(
            functools.partial(kernel, ns, nq),
            out_shape=pltpu.VMEM(environments.shape, bf16),
            in_specs=[
                pl.BlockSpec(memory_space=pltpu.HBM),
                pl.BlockSpec(memory_space=pltpu.HBM),
                pl.BlockSpec(memory_space=pltpu.SMEM),
                pl.BlockSpec(memory_space=pltpu.HBM),
            ],
            out_specs=pl.BlockSpec(memory_space=pltpu.VMEM),
            scratch_shapes=[
                vmem((2, width, width), bf16),
                vmem((W, width, width), bf16),
                vmem((W, width, width), bf16),
                vmem((2, width, width), bf16),
                vmem((width, width), bf16),
                vmem((2, width, width), bf16),
                vmem((W, 2, width, width), f32),
                vmem((W, 2, width, width), f32),
                vmem((width, width), bf16),
                dma((count,)), dma((count,)), dma((count,)), dma((count,)),
                dma((2,)), dma((2,)), dma((2,)),
            ],
            compiler_params=pltpu.CompilerParams(
                collective_id=0, has_side_effects=True, vmem_limit_bytes=60 * 2**20
            ),
            cost_estimate=pl.CostEstimate(
                flops=54 * width**3, bytes_accessed=24 * W * width * width, transcendentals=0
            ),
        )(site_tensors, environments, mpo.transpose(0, 1, 3, 4, 2), boundary)

    return jax.shard_map(
        local,
        mesh=mesh,
        in_specs=(
            P("site", None, "sector", None),
            P("site", None, "sector", None),
            P("site", None, None, None, None),
            P(None, "sector", None),
        ),
        out_specs=P("site", None, "sector", None),
        check_vma=False,
    )
```

```python
import functools

import jax
import jax.numpy as jnp
from jax import lax
from jax.experimental import pallas as pl
from jax.experimental.pallas import tpu as pltpu
from jax.sharding import PartitionSpec as P

MESH = pl.DeviceIdType.MESH
charge_steps = (0, 1, -1, 0, 0)
W = len(charge_steps)
ORDER = (1, 0, 3, 4, 2)
DEPTH = 5


def uses(w, t, x):
    return [v for v in range(W) if t - x == charge_steps[v] - charge_steps[w]]


def dot(a, b):
    return jnp.dot(a, b, preferred_element_type=jnp.float32)


def chunks_of(width):
    cut = width - width // 3
    return [(w, 0, cut) for w in ORDER] + [(w, cut, width - cut) for w in ORDER]


def kernel(
    ns, nq, site_hbm, env, mpo, bnd, out,
    site, inc, low, below_site, above_site, flip, total, part, pair_out,
    env_send, env_recv, relay_send, relay_recv, near_send, near_recv, local_sem,
):
    s = lax.axis_index("site")
    q = lax.axis_index("sector")
    nxt, prv = lax.rem(s + 1, ns), lax.rem(s + ns - 1, ns)
    above, below = lax.rem(q + 1, nq), lax.rem(q + nq - 1, nq)
    has_next, has_prev = s < ns - 1, s > 0
    width = site.shape[-1]
    chunks = chunks_of(width)
    count = len(chunks)

    def at(place, sector):
        return {"site": place, "sector": sector}

    own_copy = pltpu.make_async_copy(site_hbm.at[0], site, local_sem.at[0])
    own_copy.start()
    bnd_copy = pltpu.make_async_copy(bnd, inc, local_sem.at[1])

    @pl.when(jnp.logical_not(has_prev))
    def _():
        bnd_copy.start()

    barrier = pltpu.get_barrier_semaphore()
    for other in (above, below):
        pl.semaphore_signal(barrier, inc=1, device_id=at(s, other), device_id_type=MESH)

    @pl.when(has_next)
    def _():
        pl.semaphore_signal(barrier, inc=1, device_id=at(nxt, q), device_id_type=MESH)

    @pl.when(has_prev)
    def _():
        pl.semaphore_signal(barrier, inc=1, device_id=at(prv, q), device_id_type=MESH)

    pl.semaphore_wait(barrier, 2 + has_next.astype(jnp.int32) + has_prev.astype(jnp.int32))

    def env_copy(k):
        w, row, rows = chunks[k]
        return pltpu.make_async_remote_copy(
            src_ref=env.at[0, w, pl.ds(row, rows)], dst_ref=inc.at[w, pl.ds(row, rows)],
            send_sem=env_send.at[k], recv_sem=env_recv.at[k],
            device_id=at(nxt, q), device_id_type=MESH,
        )

    def relay_copy(k):
        w, row, rows = chunks[k]
        source = (pair_out if charge_steps[w] < 0 else inc.at[w]).at[pl.ds(row, rows)]
        return pltpu.make_async_remote_copy(
            src_ref=source, dst_ref=low.at[w, pl.ds(row, rows)],
            send_sem=relay_send.at[k], recv_sem=relay_recv.at[k],
            device_id=at(s, above), device_id_type=MESH,
        )

    to_below = pltpu.make_async_remote_copy(
        src_ref=site_hbm.at[0, 0], dst_ref=above_site,
        send_sem=near_send.at[0], recv_sem=near_recv.at[0],
        device_id=at(s, below), device_id_type=MESH,
    )
    to_above = pltpu.make_async_remote_copy(
        src_ref=site_hbm.at[0], dst_ref=below_site,
        send_sem=near_send.at[1], recv_sem=near_recv.at[1],
        device_id=at(s, above), device_id_type=MESH,
    )

    @pl.when(has_next)
    def _():
        for k in range(DEPTH):
            env_copy(k).start()

    to_below.start()
    to_above.start()

    own_copy.wait()
    flip[0] = site[0].T

    @pl.when(jnp.logical_not(has_prev))
    def _():
        bnd_copy.wait()

    seen, complete = {}, set()
    needed = {
        (v, x): sum(v in uses(w, t, x) for w in range(W) for t in range(2))
        for v in range(W) for x in range(2)
    }

    def add(product, k, t, x):
        w, row, rows = chunks[k]
        for v in uses(w, t, x):
            term = mpo[0, w, x, t, v] * product
            so_far = seen.get((v, x, row), 0)
            seen[v, x, row] = so_far + 1
            if so_far:
                term = total[v, x, row:row + rows] + term
            if so_far + 1 < needed[v, x]:
                total[v, x, row:row + rows] = term
                continue
            piece = dot(flip[x, :, row:row + rows], term.astype(jnp.bfloat16))
            if row:
                piece = part[v, x] + piece
            if row and v in complete:
                own_piece, carried = (part[v, 0], piece) if x else (piece, part[v, 1])
                carried = carried.astype(jnp.bfloat16).astype(jnp.float32)
                out[0, v] = (own_piece + carried).astype(jnp.bfloat16)
                continue
            part[v, x] = piece
            if row:
                complete.add(v)

    def own(k):
        w, row, rows = chunks[k]
        step = charge_steps[w]
        rows_in = inc[w, row:row + rows]
        for t in (1, 0):
            if not uses(w, t, 0) and not (step < 0 and t == 1):
                continue
            block = site[t] if step == 0 else above_site[...] if step > 0 else below_site[t]
            product = dot(rows_in, block)
            if step < 0 and t == 1:
                pair_out[row:row + rows] = product.astype(jnp.bfloat16)
                relay_copy(k).start()
            add(product, k, t, 0)

    def lower(k):
        w, row, rows = chunks[k]
        step = charge_steps[w]
        relay_copy(k).wait_recv()
        rows_in = low[w, row:row + rows]
        if step < 0:
            add(rows_in.astype(jnp.float32), k, 1, 1)
            return
        for t in (1, 0):
            if uses(w, t, 1):
                add(dot(rows_in, below_site[t] if step == 0 else site[t]), k, t, 1)

    for k, (w, row, rows) in enumerate(chunks):
        @pl.when(has_prev)
        def _():
            env_copy(k).wait_recv()

        if charge_steps[w] >= 0:
            relay_copy(k).start()

        if k + DEPTH < count:
            @pl.when(has_next)
            def _():
                env_copy(k).wait_send()
                env_copy(k + DEPTH).start()

        if k == 0:
            to_below.wait_recv()
            to_above.wait_recv()
            flip[1] = below_site[1].T
        own(k)
        if k:
            lower(k - 1)
    lower(count - 1)

    to_below.wait_send()
    to_above.wait_send()
    for k in range(count):
        relay_copy(k).wait_send()

    @pl.when(has_next)
    def _():
        for k in range(count - DEPTH, count):
            env_copy(k).wait_send()


def solution(mesh):
    ns, nq = mesh.shape["site"], mesh.shape["sector"]

    def local(site_tensors, environments, mpo, boundary):
        width = site_tensors.shape[3]
        count = len(chunks_of(width))
        vmem, dma = pltpu.VMEM, pltpu.SemaphoreType.DMA
        bf16, f32 = jnp.bfloat16, jnp.float32
        return pl.pallas_call(
            functools.partial(kernel, ns, nq),
            out_shape=pltpu.VMEM(environments.shape, bf16),
            in_specs=[
                pl.BlockSpec(memory_space=pltpu.HBM),
                pl.BlockSpec(memory_space=pltpu.HBM),
                pl.BlockSpec(memory_space=pltpu.SMEM),
                pl.BlockSpec(memory_space=pltpu.HBM),
            ],
            out_specs=pl.BlockSpec(memory_space=pltpu.VMEM),
            scratch_shapes=[
                vmem((2, width, width), bf16),
                vmem((W, width, width), bf16),
                vmem((W, width, width), bf16),
                vmem((2, width, width), bf16),
                vmem((width, width), bf16),
                vmem((2, width, width), bf16),
                vmem((W, 2, width, width), f32),
                vmem((W, 2, width, width), f32),
                vmem((width, width), bf16),
                dma((count,)), dma((count,)), dma((count,)), dma((count,)),
                dma((2,)), dma((2,)), dma((2,)),
            ],
            compiler_params=pltpu.CompilerParams(
                collective_id=0, has_side_effects=True, vmem_limit_bytes=60 * 2**20
            ),
            cost_estimate=pl.CostEstimate(
                flops=54 * width**3, bytes_accessed=24 * W * width * width, transcendentals=0
            ),
        )(site_tensors, environments, mpo.transpose(0, 1, 3, 4, 2), boundary)

    return jax.shard_map(
        local,
        mesh=mesh,
        in_specs=(
            P("site", None, "sector", None),
            P("site", None, "sector", None),
            P("site", None, None, None, None),
            P(None, "sector", None),
        ),
        out_specs=P("site", None, "sector", None),
        check_vma=False,
    )
```

```python
import functools

import jax
import jax.numpy as jnp
from jax import lax
from jax.experimental import pallas as pl
from jax.experimental.pallas import tpu as pltpu
from jax.sharding import PartitionSpec as P

MESH = pl.DeviceIdType.MESH
charge_steps = (0, 1, -1, 0, 0)
W = len(charge_steps)
ORDER = (1, 0, 3, 4, 2)
DEPTH = 2


def uses(w, t, x):
    return [v for v in range(W) if t - x == charge_steps[v] - charge_steps[w]]


def dot(a, b):
    return jnp.dot(a, b, preferred_element_type=jnp.float32)


def chunks_of(width):
    cut = width - width // 3
    return [(w, 0, cut) for w in ORDER] + [(w, cut, width - cut) for w in ORDER]


def kernel(
    ns, nq, site_hbm, env, mpo, bnd, out,
    site, inc, low, below_site, above_site, flip, total, part, pair_out,
    env_send, env_recv, relay_send, relay_recv, near_send, near_recv, local_sem,
):
    s = lax.axis_index("site")
    q = lax.axis_index("sector")
    nxt, prv = lax.rem(s + 1, ns), lax.rem(s + ns - 1, ns)
    above, below = lax.rem(q + 1, nq), lax.rem(q + nq - 1, nq)
    has_next, has_prev = s < ns - 1, s > 0
    width = site.shape[-1]
    chunks = chunks_of(width)
    count = len(chunks)

    def at(place, sector):
        return {"site": place, "sector": sector}

    own_copy = pltpu.make_async_copy(site_hbm.at[0], site, local_sem.at[0])
    own_copy.start()
    bnd_copy = pltpu.make_async_copy(bnd, inc, local_sem.at[1])

    @pl.when(jnp.logical_not(has_prev))
    def _():
        bnd_copy.start()

    barrier = pltpu.get_barrier_semaphore()
    for other in (above, below):
        pl.semaphore_signal(barrier, inc=1, device_id=at(s, other), device_id_type=MESH)

    @pl.when(has_next)
    def _():
        pl.semaphore_signal(barrier, inc=1, device_id=at(nxt, q), device_id_type=MESH)

    @pl.when(has_prev)
    def _():
        pl.semaphore_signal(barrier, inc=1, device_id=at(prv, q), device_id_type=MESH)

    pl.semaphore_wait(barrier, 2 + has_next.astype(jnp.int32) + has_prev.astype(jnp.int32))

    def env_copy(k):
        w, row, rows = chunks[k]
        return pltpu.make_async_remote_copy(
            src_ref=env.at[0, w, pl.ds(row, rows)], dst_ref=inc.at[w, pl.ds(row, rows)],
            send_sem=env_send.at[k], recv_sem=env_recv.at[k],
            device_id=at(nxt, q), device_id_type=MESH,
        )

    def relay_copy(k):
        w, row, rows = chunks[k]
        source = (pair_out if charge_steps[w] < 0 else inc.at[w]).at[pl.ds(row, rows)]
        return pltpu.make_async_remote_copy(
            src_ref=source, dst_ref=low.at[w, pl.ds(row, rows)],
            send_sem=relay_send.at[k], recv_sem=relay_recv.at[k],
            device_id=at(s, above), device_id_type=MESH,
        )

    to_below = pltpu.make_async_remote_copy(
        src_ref=site_hbm.at[0, 0], dst_ref=above_site,
        send_sem=near_send.at[0], recv_sem=near_recv.at[0],
        device_id=at(s, below), device_id_type=MESH,
    )
    to_above = pltpu.make_async_remote_copy(
        src_ref=site_hbm.at[0], dst_ref=below_site,
        send_sem=near_send.at[1], recv_sem=near_recv.at[1],
        device_id=at(s, above), device_id_type=MESH,
    )

    @pl.when(has_next)
    def _():
        for k in range(DEPTH):
            env_copy(k).start()

    to_below.start()
    to_above.start()

    own_copy.wait()
    flip[0] = site[0].T

    @pl.when(jnp.logical_not(has_prev))
    def _():
        bnd_copy.wait()

    seen, complete = {}, set()
    needed = {
        (v, x): sum(v in uses(w, t, x) for w in range(W) for t in range(2))
        for v in range(W) for x in range(2)
    }

    def add(product, k, t, x):
        w, row, rows = chunks[k]
        for v in uses(w, t, x):
            term = mpo[0, w, x, t, v] * product
            so_far = seen.get((v, x, row), 0)
            seen[v, x, row] = so_far + 1
            if so_far:
                term = total[v, x, row:row + rows] + term
            if so_far + 1 < needed[v, x]:
                total[v, x, row:row + rows] = term
                continue
            piece = dot(flip[x, :, row:row + rows], term.astype(jnp.bfloat16))
            if row:
                piece = part[v, x] + piece
            if row and v in complete:
                own_piece, carried = (part[v, 0], piece) if x else (piece, part[v, 1])
                carried = carried.astype(jnp.bfloat16).astype(jnp.float32)
                out[0, v] = (own_piece + carried).astype(jnp.bfloat16)
                continue
            part[v, x] = piece
            if row:
                complete.add(v)

    def own(k):
        w, row, rows = chunks[k]
        step = charge_steps[w]
        rows_in = inc[w, row:row + rows]
        for t in (1, 0):
            if not uses(w, t, 0) and not (step < 0 and t == 1):
                continue
            block = site[t] if step == 0 else above_site[...] if step > 0 else below_site[t]
            product = dot(rows_in, block)
            if step < 0 and t == 1:
                pair_out[row:row + rows] = product.astype(jnp.bfloat16)
                relay_copy(k).start()
            add(product, k, t, 0)

    def lower(k):
        w, row, rows = chunks[k]
        step = charge_steps[w]
        relay_copy(k).wait_recv()
        rows_in = low[w, row:row + rows]
        if step < 0:
            add(rows_in.astype(jnp.float32), k, 1, 1)
            return
        for t in (1, 0):
            if uses(w, t, 1):
                add(dot(rows_in, below_site[t] if step == 0 else site[t]), k, t, 1)

    for k, (w, row, rows) in enumerate(chunks):
        @pl.when(has_prev)
        def _():
            env_copy(k).wait_recv()

        if charge_steps[w] >= 0:
            relay_copy(k).start()

        if k + DEPTH < count:
            @pl.when(has_next)
            def _():
                env_copy(k).wait_send()
                env_copy(k + DEPTH).start()

        if k == 0:
            to_below.wait_recv()
            to_above.wait_recv()
            flip[1] = below_site[1].T
        own(k)
        if k:
            lower(k - 1)
    lower(count - 1)

    to_below.wait_send()
    to_above.wait_send()
    for k in range(count):
        relay_copy(k).wait_send()

    @pl.when(has_next)
    def _():
        for k in range(count - DEPTH, count):
            env_copy(k).wait_send()


def solution(mesh):
    ns, nq = mesh.shape["site"], mesh.shape["sector"]

    def local(site_tensors, environments, mpo, boundary):
        width = site_tensors.shape[3]
        count = len(chunks_of(width))
        vmem, dma = pltpu.VMEM, pltpu.SemaphoreType.DMA
        bf16, f32 = jnp.bfloat16, jnp.float32
        return pl.pallas_call(
            functools.partial(kernel, ns, nq),
            out_shape=pltpu.VMEM(environments.shape, bf16),
            in_specs=[
                pl.BlockSpec(memory_space=pltpu.HBM),
                pl.BlockSpec(memory_space=pltpu.HBM),
                pl.BlockSpec(memory_space=pltpu.SMEM),
                pl.BlockSpec(memory_space=pltpu.HBM),
            ],
            out_specs=pl.BlockSpec(memory_space=pltpu.VMEM),
            scratch_shapes=[
                vmem((2, width, width), bf16),
                vmem((W, width, width), bf16),
                vmem((W, width, width), bf16),
                vmem((2, width, width), bf16),
                vmem((width, width), bf16),
                vmem((2, width, width), bf16),
                vmem((W, 2, width, width), f32),
                vmem((W, 2, width, width), f32),
                vmem((width, width), bf16),
                dma((count,)), dma((count,)), dma((count,)), dma((count,)),
                dma((2,)), dma((2,)), dma((2,)),
            ],
            compiler_params=pltpu.CompilerParams(
                collective_id=0, has_side_effects=True, vmem_limit_bytes=60 * 2**20
            ),
            cost_estimate=pl.CostEstimate(
                flops=54 * width**3, bytes_accessed=24 * W * width * width, transcendentals=0
            ),
        )(site_tensors, environments, mpo.transpose(0, 1, 3, 4, 2), boundary)

    return jax.shard_map(
        local,
        mesh=mesh,
        in_specs=(
            P("site", None, "sector", None),
            P("site", None, "sector", None),
            P("site", None, None, None, None),
            P(None, "sector", None),
        ),
        out_specs=P("site", None, "sector", None),
        check_vma=False,
    )
```
